32 devices in a mesh: groups: 2 (over x), tp: 16 (over z, y, core).
Axes of the slice: x: 2, y: 2, z: 4, core: 2. Of those that a mesh axis runs over, the one named last changes fastest.
Arguments:
- tokens: bfloat16 [256, 8192], P(('groups', 'tp')), parts along dimension 0, may hold values from -6 to 6
- gate_blocks: bfloat16 [128, 32, 128, 128], P('tp'), may hold values from -0.09375 to 0.09375
- gate_rows: int32 [128, 32], P('tp'), may hold values from 0 to 63, as said below
- up_blocks: bfloat16 [128, 32, 128, 128], P('tp'), may hold values from -0.09375 to 0.09375
- up_rows: int32 [128, 32], P('tp'), may hold values from 0 to 63, as said below
- down_blocks: bfloat16 [128, 32, 128, 128], P('tp'), may hold values from -0.0625 to 0.0625
- down_cols: int32 [128, 32], P('tp'), may hold values from 0 to 63, as said below
- owner: int32 [64], P('tp'), may hold values from 0 to 63, each once
Outputs:
- mixed_blocks: bfloat16 [64, 256, 128], P('tp', 'groups'), parts along dimension 1
The draws below stay inside these ranges and needn't reach their ends.
There are 2 independent parts, one for each index of `groups`. The reference program is written for one: setup_inputs(seed, part) draws one part's arguments, and reference() takes and returns one part's arrays. A program takes and returns all parts, laid end to end along the dimension named above; an argument that names none is the same for every part. Nothing has to cross between parts.
Inputs may be any that keep to these rules, and one draw needn't show every extreme that they name: `gate_rows`: each row lists 32 distinct row blocks in increasing order. `up_rows`: each row lists 32 distinct row blocks in increasing order. `down_cols`: each row lists 32 distinct output blocks in increasing order; rows 2g and 2g+1 list disjoint blocks, together all 64.
All inputs are finite; a program needn't handle non-finite values.
Results may differ from the reference program's by a relative error of at most 0.0049.
Values may be sent and summed in bfloat16 or wider, within the bound.
A program may use at most 192 MiB of HBM per device.

```python
import jax
import jax.numpy as jnp
from jax import lax

D = 8192
FF = 16384
BLOCK = 128
TOKENS = 128
KEEP = 32
HB = 128
DB = 64


def block_lists(key):
    keys = jax.random.split(key, FF // BLOCK)
    picks = jax.vmap(lambda k: jax.random.permutation(k, D // BLOCK)[:D // BLOCK // 2])(keys)
    return jnp.sort(picks, axis=1).astype(jnp.int32)


def draw_gate_rows(key, part):
    key = jax.random.fold_in(key, 11)
    return block_lists(key)


def draw_up_rows(key, part):
    key = jax.random.fold_in(key, 23)
    return block_lists(key)


def draw_down_cols(key, part):
    key = jax.random.fold_in(key, 37)
    keys = jax.random.split(key, FF // BLOCK // 2)
    perms = jax.vmap(lambda k: jax.random.permutation(k, D // BLOCK))(keys)
    half = D // BLOCK // 2
    paired = jnp.stack([perms[:, :half], perms[:, half:]], axis=1)
    return jnp.sort(paired.reshape(FF // BLOCK, half), axis=1).astype(jnp.int32)


def levels(stream_key, shape, shards, low, top_value):
    level, own = 1.0, jax.random.fold_in(stream_key, 6)
    for dim, parts in shards:
        heights = jnp.exp(jax.random.uniform(jax.random.fold_in(own, dim), (parts,), jnp.float32, low / len(shards), top_value / len(shards)))
        level = level * jnp.repeat(heights, shape[dim] // parts).reshape([-1 if axis == dim else 1 for axis in range(len(shape))])
    return level


def bell_draw(own_key, extent, spread, reach, pieces=(), dtype=jnp.bfloat16):
    array = jax.random.normal(own_key, extent, jnp.float32) * spread
    if len(pieces) > 0:
        array = levels(own_key, extent, pieces, -0.22, 0.18) * array
    return jnp.clip(array, min=-reach, max=reach).astype(dtype)


def setup_inputs(seed: int = 0, part: int = 0) -> dict:
    seeds = jax.random.split(jax.random.key(seed), 9)
    part_splits = jax.random.split(jax.random.fold_in(seeds[8], part), 9)
    tokens = bell_draw(part_splits[0], (TOKENS, D), 1.0, 6.0, ((0, 16),))
    gate_blocks = bell_draw(seeds[1], (HB, KEEP, BLOCK, BLOCK), (KEEP * BLOCK) ** -0.5, 0.09375, ((0, 16),))
    gate_rows = draw_gate_rows(jax.random.fold_in(seeds[8], 71), part)
    up_blocks = bell_draw(seeds[3], (HB, KEEP, BLOCK, BLOCK), (KEEP * BLOCK) ** -0.5, 0.09375, ((0, 16),))
    up_rows = draw_up_rows(jax.random.fold_in(seeds[8], 71), part)
    down_blocks = bell_draw(seeds[5], (HB, KEEP, BLOCK, BLOCK), (FF // 2) ** -0.5, 0.0625, ((0, 16),))
    down_cols = draw_down_cols(jax.random.fold_in(seeds[8], 71), part)
    owner = jax.random.permutation(seeds[7], DB).astype(jnp.int32)
    return dict(tokens=tokens, gate_blocks=gate_blocks, gate_rows=gate_rows, up_blocks=up_blocks, up_rows=up_rows, down_blocks=down_blocks, down_cols=down_cols, owner=owner)


def reference(tokens, gate_blocks, gate_rows, up_blocks, up_rows, down_blocks, down_cols, owner):
    blocked = tokens.reshape(TOKENS, D // BLOCK, BLOCK).astype(jnp.float32)

    def hidden_block(items):
        w_gate, r_gate, w_up, r_up = items
        gate = jnp.einsum('tkc,kcf->tf', blocked[:, r_gate], w_gate.astype(jnp.float32))
        up = jnp.einsum('tkc,kcf->tf', blocked[:, r_up], w_up.astype(jnp.float32))
        return (jax.nn.silu(gate) * up).astype(jnp.bfloat16)

    hidden = lax.map(hidden_block, (gate_blocks, gate_rows, up_blocks, up_rows))

    def add_block(total, items):
        rows_h, w_down, cols = items
        part = jnp.einsum('tf,kfc->ktc', rows_h.astype(jnp.float32), w_down.astype(jnp.float32))
        return total.at[cols].add(part), None

    start = jnp.zeros((D // BLOCK, TOKENS, BLOCK), jnp.float32)
    total, unused = lax.scan(add_block, start, (hidden, down_blocks, down_cols))
    return total[owner].astype(jnp.bfloat16)
```

```python
import functools

import jax
import jax.numpy as jnp
from jax import lax
from jax.experimental import pallas as pl
from jax.experimental.pallas import tpu as pltpu
from jax.sharding import PartitionSpec as P

MESH = pl.DeviceIdType.MESH
BF = jnp.bfloat16
F32 = jnp.float32


def kernel(
    nz, ny,
    tok_ref, grows, urows, dcols, own_ref, wg_hbm, wu_hbm, wd_hbm,
    out_ref,
    wg, wu, wd, buf, xs, hid, inv_v, inv_s, own_v, own_s,
    sib_out, sib_in, y_out, y_in, z_out, zup_in, zdn_in, fin,
    wsem, wdsem, tsem, tok_send, tok_recv,
    sib_s, sib_r, ys_s, ys_r, z_s, zup_r, zdn_r,
):
    n = nz * ny * 2
    hbl, keep, blk = wg.shape[0], wg.shape[1], wg.shape[2]
    pairs = hbl // 2
    half = tok_ref.shape[1] // (2 * blk)
    rows = tok_ref.shape[0]
    ntok = rows * n
    sp = out_ref.shape[0]

    me = lax.axis_index("tp")
    c = me % 2
    y = (me // 2) % ny
    z = me // (2 * ny)

    def at(z_, y_, c_):
        return (z_ * ny + y_) * 2 + c_

    sib = at(z, y, 1 - c)
    ynb = at(z, 1 - y, c) if ny == 2 else me
    zup = at(z + 1, y, c)
    zdn = at(z - 1, y, c)
    has_up = z + 1 < nz
    has_dn = z > 0

    def wcopy(i, j):
        src, dst = ((wg_hbm, wg), (wu_hbm, wu))[i]
        return pltpu.make_async_copy(src.at[j], dst.at[j], wsem.at[i, j])

    down_copy = pltpu.make_async_copy(wd_hbm, wd, wdsem)

    for g in range(half):
        lo = tok_ref[:, 2 * g * blk:(2 * g + 1) * blk].astype(F32)
        hi = tok_ref[:, (2 * g + 1) * blk:(2 * g + 2) * blk].astype(F32)
        buf[me, g] = jnp.concatenate([lo, hi], axis=0).astype(BF)
    lane = lax.broadcasted_iota(jnp.int32, (2 * rows, blk), 1)
    mine = jnp.zeros((2 * rows, blk), jnp.int32)
    for i in range(sp):
        mine = jnp.where(lane == me * sp + i, own_ref[i], mine)
    buf[me, half] = mine.astype(F32).astype(BF)

    barrier = pltpu.get_barrier_semaphore()

    def hello(dev):
        pl.semaphore_signal(barrier, inc=1, device_id={"tp": dev}, device_id_type=MESH)

    hello(sib)
    if ny == 2:
        hello(ynb)

    @pl.when(has_up)
    def _():
        hello(zup)

    @pl.when(has_dn)
    def _():
        hello(zdn)

    pl.semaphore_wait(barrier, ny + has_up.astype(jnp.int32) + has_dn.astype(jnp.int32))

    def tcopy(kind, slot):
        dev = (zup, zdn, ynb, sib)[kind]
        return pltpu.make_async_remote_copy(
            src_ref=buf.at[slot], dst_ref=buf.at[slot],
            send_sem=tok_send.at[kind, slot], recv_sem=tok_recv.at[slot],
            device_id={"tp": dev}, device_id_type=MESH)

    def arrived(slot):
        tcopy(3, slot).wait_recv()

    @pl.when(has_up)
    def _():
        tcopy(0, me).start()

    @pl.when(has_dn)
    def _():
        tcopy(1, me).start()

    if ny == 2:
        tcopy(2, me).start()
    tcopy(3, me).start()

    def start_w(j, _):
        wcopy(0, j).start()
        wcopy(1, j).start()
        return 0

    lax.fori_loop(0, hbl, start_w, 0)
    down_copy.start()

    row_id = lax.broadcasted_iota(jnp.int32, (8, blk), 0)
    lane8 = lax.broadcasted_iota(jnp.int32, (8, blk), 1)
    inv = jnp.zeros((8, blk), jnp.int32)

    def inv_step(k, acc):
        for j in range(hbl):
            hit = jnp.logical_and(lane8 == dcols[j, k], row_id == j // 2)
            acc = jnp.where(hit, (j % 2) * keep + k, acc)
        return acc

    inv_v[...] = lax.fori_loop(0, keep, inv_step, inv)
    inv_copy = pltpu.make_async_copy(inv_v, inv_s, tsem.at[0])
    inv_copy.start()

    def relayout(z_, y_):
        s0 = at(z_, y_, 0)
        chip = z_ * ny + y_

        def step(g, _):
            a = buf[s0, g].astype(F32)
            b = buf[s0 + 1, g].astype(F32)
            xs[2 * g, chip] = jnp.concatenate([a[:rows], b[:rows]], axis=0).astype(BF)
            xs[2 * g + 1, chip] = jnp.concatenate([a[rows:], b[rows:]], axis=0).astype(BF)
            return 0

        lax.fori_loop(0, half, step, 0, unroll=8)

    def sides(d, fn):
        @pl.when(z - d >= 0)
        def _():
            fn(z - d, 0)

        @pl.when(z + d < nz)
        def _():
            fn(z + d, 1)

    def zline(z_, from_up):
        slot = at(z_, y, c)
        arrived(slot)
        if from_up:
            @pl.when(has_dn)
            def _():
                tcopy(1, slot).start()
        else:
            @pl.when(has_up)
            def _():
                tcopy(0, slot).start()
        if ny == 2:
            tcopy(2, slot).start()
        tcopy(3, slot).start()

    def yline(z_, _):
        slot = at(z_, 1 - y, c)
        arrived(slot)
        tcopy(3, slot).start()

    def own_line(z_, _):
        arrived(at(z_, y, 1 - c))
        relayout(z_, y)

    def other_line(z_, _):
        arrived(at(z_, 1 - y, 1 - c))
        relayout(z_, 1 - y)

    def gather_step(d, _):
        sides(d, zline)

        @pl.when(d == 1)
        def _():
            if ny == 2:
                yline(z, 0)
            own_line(z, 0)

        @pl.when(d > 1)
        def _():
            if ny == 2:
                sides(d - 1, yline)
            sides(d - 1, own_line)
        return 0

    lax.fori_loop(1, nz, gather_step, 0)
    sides(nz - 1, own_line)
    if ny == 2:
        other_line(z, 0)

        def other_step(d, _):
            @pl.when(d < nz - 1)
            def _():
                sides(d, other_line)
            return 0

        lax.fori_loop(1, nz, other_step, 0)
        sides(nz - 1, yline)
        sides(nz - 1, other_line)

    own_row = buf[0, half].astype(F32)
    for s in range(1, n):
        own_row = own_row + buf[s, half].astype(F32)
    own_v[...] = own_row[:8].astype(jnp.int32)
    own_copy = pltpu.make_async_copy(own_v, own_s, tsem.at[1])
    own_copy.start()

    step_k = 8 if keep % 8 == 0 else keep

    def project(w, idx, j):
        acc = None
        for k in range(0, keep, step_k):
            lhs = jnp.concatenate(
                [xs[idx[j, k + i]].reshape(ntok, blk) for i in range(step_k)], axis=1)
            rhs = w[j, k:k + step_k].reshape(step_k * blk, blk)
            part = jnp.dot(lhs, rhs, preferred_element_type=F32)
            acc = part if acc is None else acc + part
        return acc

    def hidden_step(j, _):
        wcopy(0, j).wait()
        wcopy(1, j).wait()
        gate = project(wg, grows, j)
        up = project(wu, urows, j)
        hid[j] = (gate / (1.0 + jnp.exp(-gate)) * up).astype(BF)
        return 0

    lax.fori_loop(0, hbl, hidden_step, 0)

    inv_copy.wait()
    own_copy.wait()
    down_copy.wait()

    def term(dev, i):
        col = jnp.clip(own_s[0, dev * sp + i], 0, 2 * half - 1)
        lhs, rhs = [], []
        for p in range(pairs):
            q = inv_s[p, col]
            lhs.append(hid[2 * p + q // keep])
            rhs.append(wd[2 * p + q // keep, q % keep])
        return jnp.dot(jnp.concatenate(lhs, axis=1), jnp.concatenate(rhs, axis=0),
                       preferred_element_type=F32)

    above = nz - 1 - z
    far = jnp.maximum(z, above)
    near = jnp.minimum(z, above)
    sign = jnp.where(above >= z, 1, -1)

    def target(t):
        u = t - (far - near)
        first = u < 0
        dist = jnp.where(first, far - t, near - u // 2)
        side = jnp.where(jnp.logical_or(first, u % 2 == 0), sign, -sign)
        return z + jnp.where(t == nz - 1, 0, side * dist)

    def scopy(k, t):
        return pltpu.make_async_remote_copy(
            src_ref=sib_out.at[k, t], dst_ref=sib_in.at[k, t],
            send_sem=sib_s.at[k, t], recv_sem=sib_r.at[k, t],
            device_id={"tp": sib}, device_id_type=MESH)

    def ycopy(t):
        return pltpu.make_async_remote_copy(
            src_ref=y_out.at[t], dst_ref=y_in.at[t],
            send_sem=ys_s.at[t], recv_sem=ys_r.at[t],
            device_id={"tp": ynb}, device_id_type=MESH)

    def zcopy(upward, t):
        return pltpu.make_async_remote_copy(
            src_ref=z_out.at[t], dst_ref=(zup_in if upward else zdn_in).at[t],
            send_sem=z_s.at[t], recv_sem=(zup_r if upward else zdn_r).at[t],
            device_id={"tp": zup if upward else zdn}, device_id_type=MESH)

    def to_sibling(k, y_):
        def step(t, _):
            t = target(t)
            for i in range(sp):
                sib_out[k, t, i] = term(at(t, y_, 1 - c), i).astype(BF)
            scopy(k, t).start()
            return 0

        lax.fori_loop(0, nz, step, 0)

    if ny == 2:
        to_sibling(0, 1 - y)

        def to_y(t, _):
            t = target(t)
            scopy(0, t).wait_recv()
            for i in range(sp):
                y_out[t, i] = (term(at(t, 1 - y, c), i) + sib_in[0, t, i].astype(F32)).astype(BF)
            ycopy(t).start()
            return 0

        lax.fori_loop(0, nz, to_y, 0)

    to_sibling(1, y)

    def to_z(t, _):
        t = target(t)
        scopy(1, t).wait_recv()
        if ny == 2:
            ycopy(t).wait_recv()
        for i in range(sp):
            total = term(at(t, y, c), i) + sib_in[1, t, i].astype(F32)
            if ny == 2:
                total = total + y_in[t, i].astype(F32)
            fin[i] = total

        @pl.when(jnp.logical_and(t >= z, has_dn))
        def _():
            zcopy(True, t).wait_recv()
            fin[...] += zup_in[t].astype(F32)

        @pl.when(jnp.logical_and(t <= z, has_up))
        def _():
            zcopy(False, t).wait_recv()
            fin[...] += zdn_in[t].astype(F32)

        @pl.when(t > z)
        def _():
            z_out[t] = fin[...].astype(BF)
            zcopy(True, t).start()

        @pl.when(t < z)
        def _():
            z_out[t] = fin[...].astype(BF)
            zcopy(False, t).start()

        @pl.when(t == z)
        def _():
            out_ref[...] = fin[...].astype(BF)
        return 0

    lax.fori_loop(0, nz, to_z, 0)

    def sent_line(slot, up, dn):
        if up is not None:
            @pl.when(up)
            def _():
                tcopy(0, slot).wait_send()
        if dn is not None:
            @pl.when(dn)
            def _():
                tcopy(1, slot).wait_send()
        if ny == 2:
            tcopy(2, slot).wait_send()
        tcopy(3, slot).wait_send()

    sent_line(me, has_up, has_dn)

    def line_sent(z_, from_up):
        sent_line(at(z_, y, c), None if from_up else has_up, has_dn if from_up else None)

    def drain(d, _):
        sides(d, line_sent)
        return 0

    lax.fori_loop(1, nz, drain, 0)

    def drain_t(t, _):
        if ny == 2:
            tcopy(3, at(t, 1 - y, c)).wait_send()
            scopy(0, t).wait_send()
            ycopy(t).wait_send()
        scopy(1, t).wait_send()

        @pl.when(t > z)
        def _():
            zcopy(True, t).wait_send()

        @pl.when(t < z)
        def _():
            zcopy(False, t).wait_send()
        return 0

    lax.fori_loop(0, nz, drain_t, 0)


def body(nz, ny, tokens, gate_blocks, gate_rows, up_blocks, up_rows, down_blocks, down_cols, owner):
    n = nz * ny * 2
    rows, width = tokens.shape
    hbl, keep, blk, _ = gate_blocks.shape
    sp = owner.shape[0]
    ntok = rows * n
    db = width // blk
    half = db // 2
    chips = n // 2
    smem = pl.BlockSpec(memory_space=pltpu.SMEM)
    vmem = pl.BlockSpec(memory_space=pltpu.VMEM)
    hbm = pl.BlockSpec(memory_space=pl.ANY)
    dma = pltpu.SemaphoreType.DMA
    part = (sp, ntok, blk)
    macs = ntok * hbl * keep * blk * blk * 3
    return pl.pallas_call(
        functools.partial(kernel, nz, ny),
        out_shape=jax.ShapeDtypeStruct(part, BF),
        in_specs=[vmem, smem, smem, smem, smem, hbm, hbm, hbm],
        out_specs=vmem,
        scratch_shapes=[
            pltpu.VMEM(gate_blocks.shape, BF),
            pltpu.VMEM(up_blocks.shape, BF),
            pltpu.VMEM(down_blocks.shape, BF),
            pltpu.VMEM((n, half + 1, 2 * rows, blk), BF),
            pltpu.VMEM((db, chips, 2 * rows, blk), BF),
            pltpu.VMEM((hbl, ntok, blk), BF),
            pltpu.VMEM((8, blk), jnp.int32),
            pltpu.SMEM((8, blk), jnp.int32),
            pltpu.VMEM((8, blk), jnp.int32),
            pltpu.SMEM((8, blk), jnp.int32),
            pltpu.VMEM((2, nz) + part, BF),
            pltpu.VMEM((2, nz) + part, BF),
            pltpu.VMEM((nz,) + part, BF),
            pltpu.VMEM((nz,) + part, BF),
            pltpu.VMEM((nz,) + part, BF),
            pltpu.VMEM((nz,) + part, BF),
            pltpu.VMEM((nz,) + part, BF),
            pltpu.VMEM(part, F32),
            dma((2, hbl)), dma(()), dma((2,)), dma((4, n)), dma((n,)),
            dma((2, nz)), dma((2, nz)), dma((nz,)), dma((nz,)),
            dma((nz,)), dma((nz,)), dma((nz,)),
        ],
        compiler_params=pltpu.CompilerParams(
            collective_id=0, has_side_effects=True, vmem_limit_bytes=58 * 1024 * 1024
        ),
        cost_estimate=pl.CostEstimate(
            flops=2 * macs, bytes_accessed=3 * gate_blocks.size * 2, transcendentals=hbl * ntok * blk
        ),
    )(tokens, gate_rows, up_rows, down_cols, owner, gate_blocks, up_blocks, down_blocks)


def line_shape(mesh):
    n = mesh.shape["tp"]
    row = mesh.devices.reshape(-1, n)[0]
    ys = [getattr(d, "coords", (0, 0, 0))[1] for d in row]
    ny = 2 if len(set(ys)) == 2 and n % 4 == 0 else 1
    return n // (2 * ny), ny


def solution(mesh):
    nz, ny = line_shape(mesh)
    in_specs = (
        P(("groups", "tp"), None),
        P("tp", None, None, None),
        P("tp", None),
        P("tp", None, None, None),
        P("tp", None),
        P("tp", None, None, None),
        P("tp", None),
        P("tp"),
    )
    out_specs = P("tp", "groups", None)
    return jax.shard_map(
        functools.partial(body, nz, ny), mesh=mesh, in_specs=in_specs, out_specs=out_specs,
        check_vma=False,
    )
```

```python
import functools

import jax
import jax.numpy as jnp
from jax import lax
from jax.experimental import pallas as pl
from jax.experimental.pallas import tpu as pltpu
from jax.sharding import PartitionSpec as P

MESH = pl.DeviceIdType.MESH
BF = jnp.bfloat16
F32 = jnp.float32


def kernel(
    nz, ny,
    tok_ref, grows, urows, dcols, own_ref, wg_hbm, wu_hbm, wd_hbm,
    out_ref,
    wg, wu, wd, buf, xs, hid, inv_v, inv_s, own_v, own_s,
    sib_out, sib_in, y_out, y_in, z_out, zup_in, zdn_in, fin,
    wsem, wdsem, tsem, tok_send, tok_recv,
    sib_s, sib_r, ys_s, ys_r, z_s, zup_r, zdn_r,
):
    n = nz * ny * 2
    hbl, keep, blk = wg.shape[0], wg.shape[1], wg.shape[2]
    pairs = hbl // 2
    half = tok_ref.shape[1] // (2 * blk)
    rows = tok_ref.shape[0]
    ntok = rows * n
    sp = out_ref.shape[0]

    me = lax.axis_index("tp")
    c = me % 2
    y = (me // 2) % ny
    z = me // (2 * ny)

    def at(z_, y_, c_):
        return (z_ * ny + y_) * 2 + c_

    sib = at(z, y, 1 - c)
    ynb = at(z, 1 - y, c) if ny == 2 else me
    zup = at(z + 1, y, c)
    zdn = at(z - 1, y, c)
    has_up = z + 1 < nz
    has_dn = z > 0

    def wcopy(i, j):
        src, dst = ((wg_hbm, wg), (wu_hbm, wu))[i]
        return pltpu.make_async_copy(src.at[j], dst.at[j], wsem.at[i, j])

    down_copy = pltpu.make_async_copy(wd_hbm, wd, wdsem)

    barrier = pltpu.get_barrier_semaphore()

    def hello(dev):
        pl.semaphore_signal(barrier, inc=1, device_id={"tp": dev}, device_id_type=MESH)

    hello(sib)
    if ny == 2:
        hello(ynb)

    @pl.when(has_up)
    def _():
        hello(zup)

    @pl.when(has_dn)
    def _():
        hello(zdn)

    for g in range(half):
        lo = tok_ref[:, 2 * g * blk:(2 * g + 1) * blk].astype(F32)
        hi = tok_ref[:, (2 * g + 1) * blk:(2 * g + 2) * blk].astype(F32)
        buf[me, g] = jnp.concatenate([lo, hi], axis=0).astype(BF)
    lane = lax.broadcasted_iota(jnp.int32, (2 * rows, blk), 1)
    mine = jnp.zeros((2 * rows, blk), jnp.int32)
    for i in range(sp):
        mine = jnp.where(lane == me * sp + i, own_ref[i], mine)
    buf[me, half] = mine.astype(F32).astype(BF)

    pl.semaphore_wait(barrier, ny + has_up.astype(jnp.int32) + has_dn.astype(jnp.int32))

    def tcopy(kind, slot):
        dev = (zup, zdn, ynb, sib)[kind]
        return pltpu.make_async_remote_copy(
            src_ref=buf.at[slot], dst_ref=buf.at[slot],
            send_sem=tok_send.at[kind, slot], recv_sem=tok_recv.at[slot],
            device_id={"tp": dev}, device_id_type=MESH)

    def arrived(slot):
        tcopy(3, slot).wait_recv()

    @pl.when(has_up)
    def _():
        tcopy(0, me).start()

    @pl.when(has_dn)
    def _():
        tcopy(1, me).start()

    if ny == 2:
        tcopy(2, me).start()
    tcopy(3, me).start()

    def start_w(j, _):
        wcopy(0, j).start()
        wcopy(1, j).start()
        return 0

    lax.fori_loop(0, hbl, start_w, 0)
    down_copy.start()

    row_id = lax.broadcasted_iota(jnp.int32, (8, blk), 0)
    lane8 = lax.broadcasted_iota(jnp.int32, (8, blk), 1)
    inv = jnp.zeros((8, blk), jnp.int32)

    def inv_step(k, acc):
        for j in range(hbl):
            hit = jnp.logical_and(lane8 == dcols[j, k], row_id == j // 2)
            acc = jnp.where(hit, (j % 2) * keep + k, acc)
        return acc

    inv_v[...] = lax.fori_loop(0, keep, inv_step, inv)
    inv_copy = pltpu.make_async_copy(inv_v, inv_s, tsem.at[0])
    inv_copy.start()

    def relayout(z_, y_):
        s0 = at(z_, y_, 0)
        chip = z_ * ny + y_

        def step(g, _):
            a = buf[s0, g].astype(F32)
            b = buf[s0 + 1, g].astype(F32)
            xs[2 * g, chip] = jnp.concatenate([a[:rows], b[:rows]], axis=0).astype(BF)
            xs[2 * g + 1, chip] = jnp.concatenate([a[rows:], b[rows:]], axis=0).astype(BF)
            return 0

        lax.fori_loop(0, half, step, 0, unroll=8)

    def sides(d, fn):
        @pl.when(z - d >= 0)
        def _():
            fn(z - d, 0)

        @pl.when(z + d < nz)
        def _():
            fn(z + d, 1)

    def zline(z_, from_up):
        slot = at(z_, y, c)
        arrived(slot)
        if from_up:
            @pl.when(has_dn)
            def _():
                tcopy(1, slot).start()
        else:
            @pl.when(has_up)
            def _():
                tcopy(0, slot).start()
        if ny == 2:
            tcopy(2, slot).start()
        tcopy(3, slot).start()

    def yline(z_, _):
        slot = at(z_, 1 - y, c)
        arrived(slot)
        tcopy(3, slot).start()

    def own_line(z_, _):
        arrived(at(z_, y, 1 - c))
        relayout(z_, y)

    def other_line(z_, _):
        arrived(at(z_, 1 - y, 1 - c))
        relayout(z_, 1 - y)

    def gather_step(d, _):
        sides(d, zline)

        @pl.when(d == 1)
        def _():
            if ny == 2:
                yline(z, 0)
            own_line(z, 0)

        @pl.when(d > 1)
        def _():
            if ny == 2:
                sides(d - 1, yline)
            sides(d - 1, own_line)
        return 0

    lax.fori_loop(1, nz, gather_step, 0)
    sides(nz - 1, own_line)
    if ny == 2:
        other_line(z, 0)

        def other_step(d, _):
            @pl.when(d < nz - 1)
            def _():
                sides(d, other_line)
            return 0

        lax.fori_loop(1, nz, other_step, 0)
        sides(nz - 1, yline)
        sides(nz - 1, other_line)

    own_row = buf[0, half].astype(F32)
    for s in range(1, n):
        own_row = own_row + buf[s, half].astype(F32)
    own_v[...] = own_row[:8].astype(jnp.int32)
    own_copy = pltpu.make_async_copy(own_v, own_s, tsem.at[1])
    own_copy.start()

    step_k = 8 if keep % 8 == 0 else keep

    def project(w, idx, j):
        acc = None
        for k in range(0, keep, step_k):
            lhs = jnp.concatenate(
                [xs[idx[j, k + i]].reshape(ntok, blk) for i in range(step_k)], axis=1)
            rhs = w[j, k:k + step_k].reshape(step_k * blk, blk)
            part = jnp.dot(lhs, rhs, preferred_element_type=F32)
            acc = part if acc is None else acc + part
        return acc

    def hidden_step(j, _):
        wcopy(0, j).wait()
        wcopy(1, j).wait()
        gate = project(wg, grows, j)
        up = project(wu, urows, j)
        hid[j] = (gate / (1.0 + jnp.exp(-gate)) * up).astype(BF)
        return 0

    lax.fori_loop(0, hbl, hidden_step, 0)

    inv_copy.wait()
    own_copy.wait()
    down_copy.wait()

    def term(dev, i):
        col = jnp.clip(own_s[0, dev * sp + i], 0, 2 * half - 1)
        lhs, rhs = [], []
        for p in range(pairs):
            q = inv_s[p, col]
            lhs.append(hid[2 * p + q // keep])
            rhs.append(wd[2 * p + q // keep, q % keep])
        return jnp.dot(jnp.concatenate(lhs, axis=1), jnp.concatenate(rhs, axis=0),
                       preferred_element_type=F32)

    above = nz - 1 - z
    far = jnp.maximum(z, above)
    near = jnp.minimum(z, above)
    sign = jnp.where(above >= z, 1, -1)

    def target(t):
        u = t - (far - near)
        first = u < 0
        dist = jnp.where(first, far - t, near - u // 2)
        side = jnp.where(jnp.logical_or(first, u % 2 == 0), sign, -sign)
        return z + jnp.where(t == nz - 1, 0, side * dist)

    def scopy(k, t):
        return pltpu.make_async_remote_copy(
            src_ref=sib_out.at[k, t], dst_ref=sib_in.at[k, t],
            send_sem=sib_s.at[k, t], recv_sem=sib_r.at[k, t],
            device_id={"tp": sib}, device_id_type=MESH)

    def ycopy(t):
        return pltpu.make_async_remote_copy(
            src_ref=y_out.at[t], dst_ref=y_in.at[t],
            send_sem=ys_s.at[t], recv_sem=ys_r.at[t],
            device_id={"tp": ynb}, device_id_type=MESH)

    def zcopy(upward, t):
        return pltpu.make_async_remote_copy(
            src_ref=z_out.at[t], dst_ref=(zup_in if upward else zdn_in).at[t],
            send_sem=z_s.at[t], recv_sem=(zup_r if upward else zdn_r).at[t],
            device_id={"tp": zup if upward else zdn}, device_id_type=MESH)

    def to_sibling(k, y_):
        def step(t, _):
            t = target(t)
            for i in range(sp):
                sib_out[k, t, i] = term(at(t, y_, 1 - c), i).astype(BF)
            scopy(k, t).start()
            return 0

        lax.fori_loop(0, nz, step, 0)

    if ny == 2:
        to_sibling(0, 1 - y)

        def to_y(t, _):
            t = target(t)
            scopy(0, t).wait_recv()
            for i in range(sp):
                y_out[t, i] = (term(at(t, 1 - y, c), i) + sib_in[0, t, i].astype(F32)).astype(BF)
            ycopy(t).start()
            return 0

        lax.fori_loop(0, nz, to_y, 0)

    to_sibling(1, y)

    def to_z(t, _):
        t = target(t)
        scopy(1, t).wait_recv()
        if ny == 2:
            ycopy(t).wait_recv()
        for i in range(sp):
            total = term(at(t, y, c), i) + sib_in[1, t, i].astype(F32)
            if ny == 2:
                total = total + y_in[t, i].astype(F32)
            fin[i] = total

        @pl.when(jnp.logical_and(t >= z, has_dn))
        def _():
            zcopy(True, t).wait_recv()
            fin[...] += zup_in[t].astype(F32)

        @pl.when(jnp.logical_and(t <= z, has_up))
        def _():
            zcopy(False, t).wait_recv()
            fin[...] += zdn_in[t].astype(F32)

        @pl.when(t > z)
        def _():
            z_out[t] = fin[...].astype(BF)
            zcopy(True, t).start()

        @pl.when(t < z)
        def _():
            z_out[t] = fin[...].astype(BF)
            zcopy(False, t).start()

        @pl.when(t == z)
        def _():
            out_ref[...] = fin[...].astype(BF)
        return 0

    lax.fori_loop(0, nz, to_z, 0)

    def sent_line(slot, up, dn):
        if up is not None:
            @pl.when(up)
            def _():
                tcopy(0, slot).wait_send()
        if dn is not None:
            @pl.when(dn)
            def _():
                tcopy(1, slot).wait_send()
        if ny == 2:
            tcopy(2, slot).wait_send()
        tcopy(3, slot).wait_send()

    sent_line(me, has_up, has_dn)

    def line_sent(z_, from_up):
        sent_line(at(z_, y, c), None if from_up else has_up, has_dn if from_up else None)

    def drain(d, _):
        sides(d, line_sent)
        return 0

    lax.fori_loop(1, nz, drain, 0)

    def drain_t(t, _):
        if ny == 2:
            tcopy(3, at(t, 1 - y, c)).wait_send()
            scopy(0, t).wait_send()
            ycopy(t).wait_send()
        scopy(1, t).wait_send()

        @pl.when(t > z)
        def _():
            zcopy(True, t).wait_send()

        @pl.when(t < z)
        def _():
            zcopy(False, t).wait_send()
        return 0

    lax.fori_loop(0, nz, drain_t, 0)


def body(nz, ny, tokens, gate_blocks, gate_rows, up_blocks, up_rows, down_blocks, down_cols, owner):
    n = nz * ny * 2
    rows, width = tokens.shape
    hbl, keep, blk, _ = gate_blocks.shape
    sp = owner.shape[0]
    ntok = rows * n
    db = width // blk
    half = db // 2
    chips = n // 2
    smem = pl.BlockSpec(memory_space=pltpu.SMEM)
    vmem = pl.BlockSpec(memory_space=pltpu.VMEM)
    hbm = pl.BlockSpec(memory_space=pl.ANY)
    dma = pltpu.SemaphoreType.DMA
    part = (sp, ntok, blk)
    macs = ntok * hbl * keep * blk * blk * 3
    return pl.pallas_call(
        functools.partial(kernel, nz, ny),
        out_shape=jax.ShapeDtypeStruct(part, BF),
        in_specs=[vmem, smem, smem, smem, smem, hbm, hbm, hbm],
        out_specs=vmem,
        scratch_shapes=[
            pltpu.VMEM(gate_blocks.shape, BF),
            pltpu.VMEM(up_blocks.shape, BF),
            pltpu.VMEM(down_blocks.shape, BF),
            pltpu.VMEM((n, half + 1, 2 * rows, blk), BF),
            pltpu.VMEM((db, chips, 2 * rows, blk), BF),
            pltpu.VMEM((hbl, ntok, blk), BF),
            pltpu.VMEM((8, blk), jnp.int32),
            pltpu.SMEM((8, blk), jnp.int32),
            pltpu.VMEM((8, blk), jnp.int32),
            pltpu.SMEM((8, blk), jnp.int32),
            pltpu.VMEM((2, nz) + part, BF),
            pltpu.VMEM((2, nz) + part, BF),
            pltpu.VMEM((nz,) + part, BF),
            pltpu.VMEM((nz,) + part, BF),
            pltpu.VMEM((nz,) + part, BF),
            pltpu.VMEM((nz,) + part, BF),
            pltpu.VMEM((nz,) + part, BF),
            pltpu.VMEM(part, F32),
            dma((2, hbl)), dma(()), dma((2,)), dma((4, n)), dma((n,)),
            dma((2, nz)), dma((2, nz)), dma((nz,)), dma((nz,)),
            dma((nz,)), dma((nz,)), dma((nz,)),
        ],
        compiler_params=pltpu.CompilerParams(
            collective_id=0, has_side_effects=True, vmem_limit_bytes=58 * 1024 * 1024
        ),
        cost_estimate=pl.CostEstimate(
            flops=2 * macs, bytes_accessed=3 * gate_blocks.size * 2, transcendentals=hbl * ntok * blk
        ),
    )(tokens, gate_rows, up_rows, down_cols, owner, gate_blocks, up_blocks, down_blocks)


def line_shape(mesh):
    n = mesh.shape["tp"]
    row = mesh.devices.reshape(-1, n)[0]
    ys = [getattr(d, "coords", (0, 0, 0))[1] for d in row]
    ny = 2 if len(set(ys)) == 2 and n % 4 == 0 else 1
    return n // (2 * ny), ny


def solution(mesh):
    nz, ny = line_shape(mesh)
    in_specs = (
        P(("groups", "tp"), None),
        P("tp", None, None, None),
        P("tp", None),
        P("tp", None, None, None),
        P("tp", None),
        P("tp", None, None, None),
        P("tp", None),
        P("tp"),
    )
    out_specs = P("tp", "groups", None)
    return jax.shard_map(
        functools.partial(body, nz, ny), mesh=mesh, in_specs=in_specs, out_specs=out_specs,
        check_vma=False,
    )
```
